32 devices in a mesh: row: 8 (over z, y), col: 4 (over x, core).
Axes of the slice: x: 2, y: 2, z: 4, core: 2. Of those that a mesh axis runs over, the one named last changes fastest.
Arguments:
- factors: bfloat16 [768, 12, 5120], P('row', None, 'col'), may hold values from -0.21875 to 0.21875
- amplitudes: bfloat16 [4, 12, 12], replicated, may hold values from -6 to 6
- vir_energy: float32 [768], replicated, may hold values from 0.2 to 2
- pair_energy: float32 [4], replicated, may hold values from -1.5 to -0.5
Outputs:
- residual: float32 [4, 768, 768], P('col', 'row')
- update: float32 [4, 768, 768], P('col', 'row')
The draws below stay inside these ranges and needn't reach their ends.
All inputs are finite; a program needn't handle non-finite values.
Results may differ from the reference program's by a relative error of at most 0.0024.
Values may be sent and summed in bfloat16 or wider, within the bound.
A program may use at most 256 MiB of HBM per device.

```python
import jax
import jax.numpy as jnp
from jax import lax

V = 768
Q = 5120
S = 12
P_SIZE = 4
VIR_ROW = 96
AUX_COL = 1280
N_ROW = 8
N_COL = 4


def steps_of(rng, extent, cuts, smallest, top_value):
    level, own = 1.0, jax.random.fold_in(rng, 6)
    for axis_at, blocks in cuts:
        heights = jnp.exp(jax.random.uniform(jax.random.fold_in(own, axis_at), (blocks,), jnp.float32, smallest / len(cuts), top_value / len(cuts)))
        level = level * jnp.repeat(heights, extent[axis_at] // blocks).reshape([-1 if axis == axis_at else 1 for axis in range(len(extent))])
    return level


def gaussian(rng, dims, deviation, most, shards=(), kind=jnp.bfloat16):
    array = jax.random.normal(rng, dims, jnp.float32) * deviation
    if len(shards) > 0:
        array = steps_of(rng, dims, shards, -0.22, 0.18) * array
    return jnp.clip(array, min=-most, max=most).astype(kind)


def setup_inputs(seed: int = 0) -> dict:
    splits = jax.random.split(jax.random.key(seed), 5)
    return {
        "factors": gaussian(splits[0], (V, S, Q), ((S * Q ** 0.5) ** -0.5), 0.21875, ((0, 8), (2, 4))),
        "amplitudes": gaussian(splits[1], (P_SIZE, S, S), 1.0, 6.0),
        "vir_energy": jnp.clip(jax.random.uniform(splits[2], (V,), jnp.float32, 0.2, 2.0), 0.2, 2.0),
        "pair_energy": jnp.clip(jax.random.uniform(splits[3], (P_SIZE,), jnp.float32, -1.5, -0.5), -1.5, -0.5),
    }


def reference(factors, amplitudes, vir_energy, pair_energy):
    aux_blocks = jnp.transpose(factors.reshape(V, S, N_COL, AUX_COL), (2, 0, 1, 3))
    wide_amplitudes = amplitudes.astype(jnp.float32)

    def block_rows(row_index):
        def add_block(total, aux_index):
            right_block = aux_blocks[aux_index]
            slab_block = lax.dynamic_slice_in_dim(right_block, (row_index * VIR_ROW).astype(jnp.int32), VIR_ROW, 0)
            products = jnp.dot(slab_block.reshape(VIR_ROW * S, AUX_COL), right_block.reshape(V * S, AUX_COL).T, preferred_element_type=jnp.float32)
            products = products.astype(jnp.bfloat16).astype(jnp.float32).reshape(VIR_ROW, S, V, S)
            term = jnp.einsum('acbd,pcd->pab', products, wide_amplitudes, precision=lax.Precision.HIGHEST)
            return total + term, None

        start = jnp.zeros((P_SIZE, VIR_ROW, V), jnp.float32)
        total, _ = lax.scan(add_block, start, jnp.arange(N_COL, dtype=jnp.int32))
        return total

    pieces = lax.map(block_rows, jnp.arange(N_ROW, dtype=jnp.int32))
    residual = jnp.transpose(pieces, (1, 0, 2, 3)).reshape(P_SIZE, V, V)
    divisor = vir_energy[None, :, None] + vir_energy[None, None, :] - pair_energy[:, None, None]
    return residual, residual / divisor
```

```python
import jax
import jax.numpy as jnp
from jax import lax
from jax.experimental import pallas as pl
from jax.experimental.pallas import tpu as pltpu
from jax.sharding import PartitionSpec as P

LANES = 128
SUB = 16
GROUP = 8


def ladder_kernel(mix_ref, block_ref, out_ref, mixed):
    slab = block_ref.shape[1]
    vir = block_ref.shape[2]
    step = pl.program_id(0)

    @pl.when(step == 0)
    def _():
        out_ref[...] = jnp.zeros_like(out_ref)

    def mix(at, carry):
        first = pl.multiple_of(at * (SUB * GROUP), SUB * GROUP)
        wide = jnp.concatenate(
            [
                block_ref[0, :, pl.ds(first + j * SUB, SUB), :].reshape(slab * SUB, LANES)
                for j in range(GROUP)
            ],
            axis=1,
        )
        result = jnp.dot(mix_ref[...], wide, preferred_element_type=jnp.float32).astype(jnp.bfloat16)
        for j in range(GROUP):
            for c in range(slab):
                mixed[pl.ds(first + j * SUB, SUB), c * LANES : (c + 1) * LANES] = result[
                    c * SUB : (c + 1) * SUB, j * LANES : (j + 1) * LANES
                ]
        return carry

    lax.fori_loop(0, vir // (SUB * GROUP), mix, 0)

    tile = 256

    def multiply(at, carry):
        first = pl.multiple_of(at * tile, tile)
        left = jnp.concatenate([block_ref[0, c, pl.ds(first, tile), :] for c in range(slab)], axis=1)
        out_ref[pl.ds(first, tile), :] += lax.dot_general(
            left, mixed[...], (((1,), (1,)), ((), ())), preferred_element_type=jnp.float32
        )
        return carry

    lax.fori_loop(0, vir // tile, multiply, 0)


def ladder(blocks, amplitudes):
    count, slab, vir, _ = blocks.shape
    mix = jnp.kron(amplitudes, jnp.eye(SUB, dtype=amplitudes.dtype))
    return pl.pallas_call(
        ladder_kernel,
        grid=(count,),
        in_specs=[
            pl.BlockSpec((slab * SUB, slab * SUB), lambda i: (0, 0)),
            pl.BlockSpec((1, slab, vir, LANES), lambda i: (i, 0, 0, 0)),
        ],
        out_specs=pl.BlockSpec((vir, vir), lambda i: (0, 0)),
        out_shape=jax.ShapeDtypeStruct((vir, vir), jnp.float32),
        scratch_shapes=[pltpu.VMEM((vir, slab * LANES), jnp.bfloat16)],
        compiler_params=pltpu.CompilerParams(vmem_limit_bytes=32 * 1024 * 1024),
        cost_estimate=pl.CostEstimate(
            flops=2 * vir * vir * slab * LANES * count,
            bytes_accessed=2 * count * slab * vir * LANES,
            transcendentals=0,
        ),
    )(mix, blocks)


def per_device(factors, amplitudes, vir_energy, pair_energy):
    row_count, slab, aux = factors.shape
    pairs = amplitudes.shape[0]
    vir = vir_energy.shape[0]
    rows = lax.axis_size("row")
    cols = lax.axis_size("col")
    here_row = lax.axis_index("row")
    here_col = lax.axis_index("col")
    share = pairs // cols
    piece = aux // rows
    depth = piece * cols

    outgoing = factors.reshape(row_count, slab, rows, piece).transpose(2, 1, 0, 3)
    swapped = lax.all_to_all(outgoing, "row", split_axis=0, concat_axis=0, tiled=True)
    gathered = lax.all_gather(swapped, "col", axis=0, tiled=False)
    whole = gathered.transpose(2, 1, 3, 0, 4).reshape(slab, vir, depth)
    mine = lax.dynamic_slice_in_dim(amplitudes, here_col * share, share, 0)
    if depth % LANES == 0 and vir % 256 == 0:
        blocks = whole.reshape(slab, vir, depth // LANES, LANES).transpose(2, 0, 1, 3)
        partial = jnp.stack([ladder(blocks, mine[p]) for p in range(share)])
    else:
        mixed = jnp.einsum(
            "pcd,dbq->pcbq", mine, whole, preferred_element_type=jnp.float32
        ).astype(jnp.bfloat16)
        partial = jnp.einsum("caq,pcbq->pab", whole, mixed, preferred_element_type=jnp.float32)
    reduced = lax.psum_scatter(partial, "row", scatter_dimension=1, tiled=True)
    first_energy = lax.dynamic_slice_in_dim(vir_energy, here_row * row_count, row_count)
    pair_here = lax.dynamic_slice_in_dim(pair_energy, here_col * share, share)
    divisor = first_energy[None, :, None] + vir_energy[None, None, :] - pair_here[:, None, None]
    return (reduced, reduced / divisor)


def solution(mesh):
    return jax.shard_map(
        per_device,
        mesh=mesh,
        in_specs=(P("row", None, "col"), P(), P(), P()),
        out_specs=(P("col", "row", None), P("col", "row", None)),
        check_vma=False,
    )
```

```python
import jax
import jax.numpy as jnp
from jax import lax
from jax.experimental import pallas as pl
from jax.experimental.pallas import tpu as pltpu
from jax.sharding import PartitionSpec as P

LANES = 128
SUB = 16
GROUP = 8


def ladder_kernel(mix_ref, block_ref, out_ref, mixed):
    slab = block_ref.shape[1]
    vir = block_ref.shape[2]
    step = pl.program_id(0)

    @pl.when(step == 0)
    def _():
        out_ref[...] = jnp.zeros_like(out_ref)

    def mix(at, carry):
        first = pl.multiple_of(at * (SUB * GROUP), SUB * GROUP)
        wide = jnp.concatenate(
            [
                block_ref[0, :, pl.ds(first + j * SUB, SUB), :].reshape(slab * SUB, LANES)
                for j in range(GROUP)
            ],
            axis=1,
        )
        result = jnp.dot(mix_ref[...], wide, preferred_element_type=jnp.float32).astype(jnp.bfloat16)
        for j in range(GROUP):
            for c in range(slab):
                mixed[pl.ds(first + j * SUB, SUB), c * LANES : (c + 1) * LANES] = result[
                    c * SUB : (c + 1) * SUB, j * LANES : (j + 1) * LANES
                ]
        return carry

    lax.fori_loop(0, vir // (SUB * GROUP), mix, 0)

    tile = 256

    def multiply(at, carry):
        first = pl.multiple_of(at * tile, tile)
        left = jnp.concatenate([block_ref[0, c, pl.ds(first, tile), :] for c in range(slab)], axis=1)
        out_ref[pl.ds(first, tile), :] += lax.dot_general(
            left, mixed[...], (((1,), (1,)), ((), ())), preferred_element_type=jnp.float32
        )
        return carry

    lax.fori_loop(0, vir // tile, multiply, 0)


def ladder(blocks, amplitudes):
    count, slab, vir, _ = blocks.shape
    mix = jnp.kron(amplitudes, jnp.eye(SUB, dtype=amplitudes.dtype))
    return pl.pallas_call(
        ladder_kernel,
        grid=(count,),
        in_specs=[
            pl.BlockSpec((slab * SUB, slab * SUB), lambda i: (0, 0)),
            pl.BlockSpec((1, slab, vir, LANES), lambda i: (i, 0, 0, 0)),
        ],
        out_specs=pl.BlockSpec((vir, vir), lambda i: (0, 0)),
        out_shape=jax.ShapeDtypeStruct((vir, vir), jnp.float32),
        scratch_shapes=[pltpu.VMEM((vir, slab * LANES), jnp.bfloat16)],
        compiler_params=pltpu.CompilerParams(vmem_limit_bytes=32 * 1024 * 1024),
        cost_estimate=pl.CostEstimate(
            flops=2 * vir * vir * slab * LANES * count,
            bytes_accessed=2 * count * slab * vir * LANES,
            transcendentals=0,
        ),
    )(mix, blocks)


def flip(index, bits):
    low, mid, high = index % 2, (index // 2) % 2, index // 4
    b0, b1, b2 = bits % 2, (bits // 2) % 2, bits // 4
    return (low + b0) % 2 + 2 * ((mid + b1) % 2) + 4 * ((high + b2) % 2)


def visit_order(step):
    return step % 2 + 4 * ((step // 2) % 2) + 2 * (step // 4)


def fused_kernel(
    mix_ref,
    blocks_ref,
    first_ref,
    second_ref,
    pair_ref,
    residual_ref,
    update_ref,
    held,
    mixed,
    partial,
    y_in,
    z_in,
    local_sem,
    row_send,
    extra_send,
    side_send,
    cross_send,
    arrive,
    y_send,
    y_arrive,
    z_send,
    z_arrive,
):
    row = lax.axis_index("row")
    col = lax.axis_index("col")
    slab, rows, row_count = held.shape[1], held.shape[2], held.shape[3]
    side = flip(col, 1)
    cross = flip(col, 2)
    corner = flip(col, 3)
    owner = row % 4

    def at(row_id, col_id):
        return (row_id, col_id)

    barrier = pltpu.get_barrier_semaphore()
    peers = [at(flip(row, j), col) for j in range(1, rows)] + [at(row, side), at(row, cross)]
    for peer in peers:
        pl.semaphore_signal(barrier, inc=1, device_id=peer, device_id_type=pl.DeviceIdType.MESH)
    pl.semaphore_wait(barrier, len(peers))

    def remote(src, dst, send, recv, device):
        return pltpu.make_async_remote_copy(
            src_ref=src,
            dst_ref=dst,
            send_sem=send,
            recv_sem=recv,
            device_id=device,
            device_id_type=pl.DeviceIdType.MESH,
        )

    def row_copy(j):
        other = flip(row, j)
        return remote(
            blocks_ref.at[other], held.at[col, :, row], row_send.at[j], arrive.at[col, row], at(other, col)
        )

    def extra_copy(e):
        return remote(
            blocks_ref.at[rows + e], held.at[4, :, row], extra_send.at[e], arrive.at[4, row], at(col + 4 * e, col)
        )

    def forward(slot, source, device, send):
        return remote(held.at[slot, :, source], held.at[slot, :, source], send, arrive.at[slot, source], device)

    def landed(slot, source):
        forward(slot, source, at(row, side), side_send.at[slot, source]).wait_recv()

    own = pltpu.make_async_copy(blocks_ref.at[row], held.at[col, :, row], local_sem.at[0])
    own.start()
    for step in range(1, rows):
        row_copy(visit_order(step)).start()
        if step in (2, 3):
            e = step - 2

            @pl.when(row != col + 4 * e)
            def _():
                extra_copy(e).start()

    @pl.when(owner == col)
    def _():
        own_extra = pltpu.make_async_copy(blocks_ref.at[rows + row // 4], held.at[4, :, row], local_sem.at[1])
        own_extra.start()
        own_extra.wait()

    own.wait()

    def mix(slot, source):
        groups = row_count // SUB
        wide = jnp.concatenate(
            [
                held[slot, :, source, j * SUB : (j + 1) * SUB, :].reshape(slab * SUB, LANES)
                for j in range(groups)
            ],
            axis=1,
        )
        result = jnp.dot(mix_ref[...], wide, preferred_element_type=jnp.float32).astype(jnp.bfloat16)
        for j in range(groups):
            for c in range(slab):
                mixed[slot, source, j * SUB : (j + 1) * SUB, c * LANES : (c + 1) * LANES] = result[
                    c * SUB : (c + 1) * SUB, j * LANES : (j + 1) * LANES
                ]

    def gather_step(step, carry):
        @pl.when(step < rows)
        def _():
            source = flip(row, visit_order(step))

            @pl.when(step > 0)
            def _():
                landed(col, source)

            forward(col, source, at(row, cross), cross_send.at[0, source]).start()
            forward(col, source, at(row, side), side_send.at[col, source]).start()

            @pl.when(owner == col)
            def _():
                @pl.when(step > 0)
                def _():
                    landed(4, source)

                forward(4, source, at(row, cross), cross_send.at[1, source]).start()
                forward(4, source, at(row, side), side_send.at[4, source]).start()

        @pl.when((step >= 1) & (step < rows + 1))
        def _():
            source = flip(row, visit_order(step - 1))
            landed(cross, source)
            forward(cross, source, at(row, side), side_send.at[cross, source]).start()

            @pl.when(owner == cross)
            def _():
                landed(4, source)
                forward(4, source, at(row, side), side_send.at[4, source]).start()

        @pl.when(step >= 2)
        def _():
            source = flip(row, visit_order(step - 2))
            landed(side, source)
            landed(corner, source)

            @pl.when((owner == side) | (owner == corner))
            def _():
                landed(4, source)

            def mix_slot(slot, inner):
                mix(slot, source)
                return inner

            lax.fori_loop(0, 5, mix_slot, 0)

        return carry

    lax.fori_loop(0, rows + 2, gather_step, 0)

    y_here, z_here = row % 2, row // 2
    y_peer = flip(row, 1)

    def tile_of(step):
        high = 1 - step // 2
        low = (step % 2 + step // 2) % 2
        return flip(z_here, 2 * high + low)

    def y_copy(tile):
        return remote(
            partial.at[tile, 1 - y_here], y_in.at[tile], y_send.at[tile], y_arrive.at[tile], at(y_peer, col)
        )

    def z_copy(tile):
        return remote(
            partial.at[tile, y_here],
            z_in.at[z_here],
            z_send.at[tile],
            z_arrive.at[z_here],
            at(2 * tile + y_here, col),
        )

    def z_landed(source):
        remote(
            partial.at[source, y_here],
            z_in.at[source],
            z_send.at[source],
            z_arrive.at[source],
            at(2 * source + y_here, col),
        ).wait_recv()

    def reduce_step(step, carry):
        @pl.when(step < 4)
        def _():
            tile = tile_of(step)

            def multiply(slot, inner):
                left = jnp.concatenate(
                    [held[slot, c, pl.ds(2 * tile, 2)].reshape(2 * row_count, LANES) for c in range(slab)], axis=1
                )
                right = mixed[slot].reshape(rows * row_count, slab * LANES)
                product = lax.dot_general(
                    left, right, (((1,), (1,)), ((), ())), preferred_element_type=jnp.float32
                ).reshape(2, row_count, rows * row_count)

                @pl.when(slot == 0)
                def _():
                    partial[tile] = product

                @pl.when(slot > 0)
                def _():
                    partial[tile] += product

                return inner

            lax.fori_loop(0, 5, multiply, 0)
            y_copy(tile).start()

        @pl.when(step >= 1)
        def _():
            tile = tile_of(step - 1)
            y_copy(tile).wait_recv()
            partial[tile, y_here] += y_in[tile]

            @pl.when(step < 4)
            def _():
                z_copy(tile).start()

        return carry

    lax.fori_loop(0, 5, reduce_step, 0)

    for j in range(1, 4):
        source = flip(z_here, j)
        z_landed(source)
        partial[z_here, y_here] += z_in[source]
    total = partial[z_here, y_here]
    residual_ref[0] = total
    update_ref[0] = total / (first_ref[...] + second_ref[...] - pair_ref[...])

    for j in range(1, rows):
        row_copy(j).wait_send()
    for e in range(2):

        @pl.when(row != col + 4 * e)
        def _():
            extra_copy(e).wait_send()

    def finish(source, carry):
        forward(col, source, at(row, cross), cross_send.at[0, source]).wait_send()
        forward(col, source, at(row, side), side_send.at[col, source]).wait_send()
        forward(cross, source, at(row, side), side_send.at[cross, source]).wait_send()

        @pl.when(owner == col)
        def _():
            forward(4, source, at(row, cross), cross_send.at[1, source]).wait_send()

        @pl.when((owner == col) | (owner == cross))
        def _():
            forward(4, source, at(row, side), side_send.at[4, source]).wait_send()

        return carry

    lax.fori_loop(0, rows, finish, 0)
    for step in range(4):
        y_copy(tile_of(step)).wait_send()
    for step in range(3):
        z_copy(tile_of(step)).wait_send()


def fused(factors, amplitudes, vir_energy, pair_energy):
    row_count, slab, aux = factors.shape
    vir = vir_energy.shape[0]
    rows = vir // row_count
    here_row = lax.axis_index("row")
    here_col = lax.axis_index("col")
    blocks = factors.reshape(row_count, slab, aux // LANES, LANES).transpose(2, 1, 0, 3)
    mine = lax.dynamic_index_in_dim(amplitudes, here_col, 0, keepdims=False)
    mix = jnp.kron(mine, jnp.eye(SUB, dtype=mine.dtype))
    first = lax.dynamic_slice_in_dim(vir_energy, here_row * row_count, row_count)[:, None]
    pair = lax.dynamic_slice_in_dim(pair_energy, here_col, 1)[:, None]
    result = jax.ShapeDtypeStruct((1, row_count, vir), jnp.float32)
    dma = pltpu.SemaphoreType.DMA
    return pl.pallas_call(
        fused_kernel,
        in_specs=[pl.BlockSpec(memory_space=pltpu.VMEM)] * 5,
        out_specs=[pl.BlockSpec(memory_space=pltpu.VMEM)] * 2,
        out_shape=[result, result],
        scratch_shapes=[
            pltpu.VMEM((5, slab, rows, row_count, LANES), jnp.bfloat16),
            pltpu.VMEM((5, rows, row_count, slab * LANES), jnp.bfloat16),
            pltpu.VMEM((rows // 2, 2, row_count, vir), jnp.float32),
            pltpu.VMEM((rows // 2, row_count, vir), jnp.float32),
            pltpu.VMEM((rows // 2, row_count, vir), jnp.float32),
            dma((2,)),
            dma((rows,)),
            dma((2,)),
            dma((5, rows)),
            dma((2, rows)),
            dma((5, rows)),
            dma((rows // 2,)),
            dma((rows // 2,)),
            dma((rows // 2,)),
            dma((rows // 2,)),
        ],
        compiler_params=pltpu.CompilerParams(
            collective_id=0, has_side_effects=True, vmem_limit_bytes=52 * 1024 * 1024
        ),
        cost_estimate=pl.CostEstimate(
            flops=2 * vir * vir * slab * LANES * 5, bytes_accessed=4 * factors.size, transcendentals=0
        ),
    )(mix, blocks, first, vir_energy[None, :], pair)


def per_device(factors, amplitudes, vir_energy, pair_energy):
    row_count, slab, aux = factors.shape
    pairs = amplitudes.shape[0]
    vir = vir_energy.shape[0]
    rows = lax.axis_size("row")
    cols = lax.axis_size("col")
    here_row = lax.axis_index("row")
    here_col = lax.axis_index("col")
    share = pairs // cols
    if rows == 8 and cols == 4 and share == 1 and aux == 10 * LANES and row_count % SUB == 0:
        return tuple(fused(factors, amplitudes, vir_energy, pair_energy))
    piece = aux // rows
    depth = piece * cols

    outgoing = factors.reshape(row_count, slab, rows, piece).transpose(2, 1, 0, 3)
    swapped = lax.all_to_all(outgoing, "row", split_axis=0, concat_axis=0, tiled=True)
    gathered = lax.all_gather(swapped, "col", axis=0, tiled=False)
    whole = gathered.transpose(2, 1, 3, 0, 4).reshape(slab, vir, depth)
    mine = lax.dynamic_slice_in_dim(amplitudes, here_col * share, share, 0)
    if depth % LANES == 0 and vir % 256 == 0:
        blocks = whole.reshape(slab, vir, depth // LANES, LANES).transpose(2, 0, 1, 3)
        partial = jnp.stack([ladder(blocks, mine[p]) for p in range(share)])
    else:
        mixed = jnp.einsum(
            "pcd,dbq->pcbq", mine, whole, preferred_element_type=jnp.float32
        ).astype(jnp.bfloat16)
        partial = jnp.einsum("caq,pcbq->pab", whole, mixed, preferred_element_type=jnp.float32)
    reduced = lax.psum_scatter(partial, "row", scatter_dimension=1, tiled=True)
    first_energy = lax.dynamic_slice_in_dim(vir_energy, here_row * row_count, row_count)
    pair_here = lax.dynamic_slice_in_dim(pair_energy, here_col * share, share)
    divisor = first_energy[None, :, None] + vir_energy[None, None, :] - pair_here[:, None, None]
    return (reduced, reduced / divisor)


def solution(mesh):
    return jax.shard_map(
        per_device,
        mesh=mesh,
        in_specs=(P("row", None, "col"), P(), P(), P()),
        out_specs=(P("col", "row", None), P("col", "row", None)),
        check_vma=False,
    )
```

```python
import jax
import jax.numpy as jnp
from jax import lax
from jax.experimental import pallas as pl
from jax.experimental.pallas import tpu as pltpu
from jax.sharding import PartitionSpec as P

LANES = 128
SUB = 16
GROUP = 8


def ladder_kernel(mix_ref, block_ref, out_ref, mixed):
    slab = block_ref.shape[1]
    vir = block_ref.shape[2]
    step = pl.program_id(0)

    @pl.when(step == 0)
    def _():
        out_ref[...] = jnp.zeros_like(out_ref)

    def mix(at, carry):
        first = pl.multiple_of(at * (SUB * GROUP), SUB * GROUP)
        wide = jnp.concatenate(
            [
                block_ref[0, :, pl.ds(first + j * SUB, SUB), :].reshape(slab * SUB, LANES)
                for j in range(GROUP)
            ],
            axis=1,
        )
        result = jnp.dot(mix_ref[...], wide, preferred_element_type=jnp.float32).astype(jnp.bfloat16)
        for j in range(GROUP):
            for c in range(slab):
                mixed[pl.ds(first + j * SUB, SUB), c * LANES : (c + 1) * LANES] = result[
                    c * SUB : (c + 1) * SUB, j * LANES : (j + 1) * LANES
                ]
        return carry

    lax.fori_loop(0, vir // (SUB * GROUP), mix, 0)

    tile = 256

    def multiply(at, carry):
        first = pl.multiple_of(at * tile, tile)
        left = jnp.concatenate([block_ref[0, c, pl.ds(first, tile), :] for c in range(slab)], axis=1)
        out_ref[pl.ds(first, tile), :] += lax.dot_general(
            left, mixed[...], (((1,), (1,)), ((), ())), preferred_element_type=jnp.float32
        )
        return carry

    lax.fori_loop(0, vir // tile, multiply, 0)


def ladder(blocks, amplitudes):
    count, slab, vir, _ = blocks.shape
    mix = jnp.kron(amplitudes, jnp.eye(SUB, dtype=amplitudes.dtype))
    return pl.pallas_call(
        ladder_kernel,
        grid=(count,),
        in_specs=[
            pl.BlockSpec((slab * SUB, slab * SUB), lambda i: (0, 0)),
            pl.BlockSpec((1, slab, vir, LANES), lambda i: (i, 0, 0, 0)),
        ],
        out_specs=pl.BlockSpec((vir, vir), lambda i: (0, 0)),
        out_shape=jax.ShapeDtypeStruct((vir, vir), jnp.float32),
        scratch_shapes=[pltpu.VMEM((vir, slab * LANES), jnp.bfloat16)],
        compiler_params=pltpu.CompilerParams(vmem_limit_bytes=32 * 1024 * 1024),
        cost_estimate=pl.CostEstimate(
            flops=2 * vir * vir * slab * LANES * count,
            bytes_accessed=2 * count * slab * vir * LANES,
            transcendentals=0,
        ),
    )(mix, blocks)


def flip(index, bits):
    low, mid, high = index % 2, (index // 2) % 2, index // 4
    b0, b1, b2 = bits % 2, (bits // 2) % 2, bits // 4
    return (low + b0) % 2 + 2 * ((mid + b1) % 2) + 4 * ((high + b2) % 2)


def fused_kernel(
    mix_ref,
    factors_ref,
    first_ref,
    second_ref,
    pair_ref,
    residual_ref,
    update_ref,
    blocks,
    packed,
    halves,
    held,
    mixed,
    partial,
    y_in,
    near_in,
    far_in,
    row_send,
    extra_send,
    side_send,
    cross_send,
    arrive,
    y_send,
    y_arrive,
    near_send,
    near_arrive,
    far_send,
    far_arrive,
):
    row = lax.axis_index("row")
    col = lax.axis_index("col")
    slab, rows, row_count = held.shape[1], held.shape[2], held.shape[3]
    side = flip(col, 1)
    cross = flip(col, 2)
    corner = flip(col, 3)
    core, x_here = col % 2, col // 2
    y_here, z_here = row % 2, row // 2
    owner = core == y_here
    half_rows = row_count // 2
    low_lane = lax.broadcasted_iota(jnp.int32, (half_rows, LANES), 1) < LANES // 2

    def swap(value):
        return pltpu.roll(value, LANES // 2, 1)

    def at(row_id, col_id):
        return (row_id, col_id)

    barrier = pltpu.get_barrier_semaphore()
    peers = [at(flip(row, j), col) for j in range(1, rows)] + [at(row, side), at(row, cross)]
    for peer in peers:
        pl.semaphore_signal(barrier, inc=1, device_id=peer, device_id_type=pl.DeviceIdType.MESH)

    for b in range(rows):
        blocks[b] = factors_ref[:, :, b * LANES : (b + 1) * LANES]
    for t in range(4):
        start = (rows + t // 2) * LANES
        for c in range(slab):
            block = factors_ref[c, :, start : start + LANES].astype(jnp.float32)
            top, bottom = block[:half_rows], block[half_rows:]
            if t % 2 == 0:
                both = jnp.where(low_lane, top, swap(bottom))
            else:
                both = jnp.where(low_lane, swap(top), bottom)
            packed[t, c] = both.astype(jnp.bfloat16)
    held[col, :, row] = blocks[row]

    @pl.when(owner)
    def _():
        halves[x_here, row] = packed[z_here]

    pl.semaphore_wait(barrier, len(peers))

    def remote(src, dst, send, recv, device):
        return pltpu.make_async_remote_copy(
            src_ref=src,
            dst_ref=dst,
            send_sem=send,
            recv_sem=recv,
            device_id=device,
            device_id_type=pl.DeviceIdType.MESH,
        )

    def row_copy(j):
        other = flip(row, j)
        return remote(
            blocks.at[other], held.at[col, :, row], row_send.at[j], arrive.at[col, row], at(other, col)
        )

    def extra_copy(d):
        target = flip(z_here, d)
        return remote(
            packed.at[target],
            halves.at[x_here, row],
            extra_send.at[d],
            arrive.at[4 + x_here, row],
            at(2 * target + core, col),
        )

    def forward(slot, source, device, send):
        return remote(held.at[slot, :, source], held.at[slot, :, source], send, arrive.at[slot, source], device)

    def forward_half(x, source, device, send):
        return remote(halves.at[x, source], halves.at[x, source], send, arrive.at[4 + x, source], device)

    def landed(slot, source):
        forward(slot, source, at(row, side), side_send.at[slot, source]).wait_recv()

    def landed_half(x, source):
        forward_half(x, source, at(row, side), side_send.at[4 + x, source]).wait_recv()

    for j in (4, 1, 2, 3):
        row_copy(j).start()

    @pl.when(jnp.logical_not(owner))
    def _():
        extra_copy(0).start()

    extra_copy(1).start()
    row_copy(5).start()
    extra_copy(2).start()

    def mix(slot, source):
        groups = row_count // SUB
        wide = jnp.concatenate(
            [
                held[slot, :, source, j * SUB : (j + 1) * SUB, :].reshape(slab * SUB, LANES)
                for j in range(groups)
            ],
            axis=1,
        )
        result = jnp.dot(mix_ref[...], wide, preferred_element_type=jnp.float32).astype(jnp.bfloat16)
        for j in range(groups):
            for c in range(slab):
                mixed[slot, source, j * SUB : (j + 1) * SUB, c * LANES : (c + 1) * LANES] = result[
                    c * SUB : (c + 1) * SUB, j * LANES : (j + 1) * LANES
                ]

    def unpack(source):
        for c in range(slab):
            first = halves[0, source, c].astype(jnp.float32)
            second = halves[1, source, c].astype(jnp.float32)
            top = jnp.where(low_lane, first, swap(second))
            bottom = jnp.where(low_lane, swap(first), second)
            held[4, c, source, :half_rows] = top.astype(jnp.bfloat16)
            held[4, c, source, half_rows:] = bottom.astype(jnp.bfloat16)

    def gather_step(step, carry):
        @pl.when(step < rows)
        def _():
            source = flip(row, step)

            @pl.when(step > 0)
            def _():
                landed(col, source)

            forward(col, source, at(row, cross), cross_send.at[0, source]).start()
            forward(col, source, at(row, side), side_send.at[col, source]).start()

            @pl.when(owner)
            def _():
                @pl.when(step > 0)
                def _():
                    landed_half(x_here, source)

                forward_half(x_here, source, at(row, cross), cross_send.at[1, source]).start()
                forward_half(x_here, source, at(row, side), side_send.at[4 + x_here, source]).start()

        @pl.when(step == 4)
        def _():
            row_copy(4).wait_send()
            row_copy(6).start()
            extra_copy(3).start()

        @pl.when(step == 5)
        def _():
            row_copy(5).wait_send()
            row_copy(7).start()

        @pl.when((step >= 1) & (step < rows + 1))
        def _():
            source = flip(row, step - 1)
            landed(cross, source)
            forward(cross, source, at(row, side), side_send.at[cross, source]).start()

            @pl.when(owner)
            def _():
                landed_half(1 - x_here, source)
                forward_half(1 - x_here, source, at(row, side), side_send.at[5 - x_here, source]).start()

        @pl.when(step >= 2)
        def _():
            source = flip(row, step - 2)
            landed(side, source)
            landed(corner, source)

            @pl.when(jnp.logical_not(owner))
            def _():
                landed_half(0, source)
                landed_half(1, source)

            unpack(source)

            def mix_slot(slot, inner):
                mix(slot, source)
                return inner

            lax.fori_loop(0, 5, mix_slot, 0)

        return carry

    lax.fori_loop(0, rows + 2, gather_step, 0)

    y_peer = flip(row, 1)

    def tile_of(step):
        return flip(z_here, 3 - step)

    def y_copy(tile):
        return remote(
            partial.at[tile, 1 - y_here], y_in.at[tile], y_send.at[tile], y_arrive.at[tile], at(y_peer, col)
        )

    def near_copy(stage):
        tile = flip(z_here, 3 - 2 * stage)
        return remote(
            partial.at[tile, y_here],
            near_in.at[stage],
            near_send.at[stage],
            near_arrive.at[stage],
            at(flip(row, 2), col),
        )

    def far_copy():
        tile = flip(z_here, 2)
        return remote(
            partial.at[tile, y_here], far_in, far_send.at[0], far_arrive.at[0], at(flip(row, 4), col)
        )

    def reduce_step(step, carry):
        @pl.when(step < 4)
        def _():
            tile = tile_of(step)

            def multiply(slot, inner):
                left = jnp.concatenate(
                    [held[slot, c, pl.ds(2 * tile, 2)].reshape(2 * row_count, LANES) for c in range(slab)], axis=1
                )
                right = mixed[slot].reshape(rows * row_count, slab * LANES)
                product = lax.dot_general(
                    left, right, (((1,), (1,)), ((), ())), preferred_element_type=jnp.float32
                ).reshape(2, row_count, rows * row_count)

                @pl.when(slot == 0)
                def _():
                    partial[tile] = product

                @pl.when(slot > 0)
                def _():
                    partial[tile] += product

                return inner

            lax.fori_loop(0, 5, multiply, 0)
            y_copy(tile).start()

        @pl.when(step >= 1)
        def _():
            tile = tile_of(step - 1)
            y_copy(tile).wait_recv()
            partial[tile, y_here] += y_in[tile]

            @pl.when(step == 1)
            def _():
                near_copy(0).start()

            @pl.when(step == 2)
            def _():
                near_copy(0).wait_recv()
                partial[tile, y_here] += near_in[0]
                far_copy().start()

            @pl.when(step == 3)
            def _():
                near_copy(1).start()

        return carry

    lax.fori_loop(0, 5, reduce_step, 0)

    near_copy(1).wait_recv()
    far_copy().wait_recv()
    total = partial[z_here, y_here] + near_in[1] + far_in[...]
    residual_ref[0] = total
    update_ref[0] = total / (first_ref[...] + second_ref[...] - pair_ref[...])

    for j in (1, 2, 3, 6, 7):
        row_copy(j).wait_send()

    @pl.when(jnp.logical_not(owner))
    def _():
        extra_copy(0).wait_send()

    for d in range(1, 4):
        extra_copy(d).wait_send()

    def finish(source, carry):
        forward(col, source, at(row, cross), cross_send.at[0, source]).wait_send()
        forward(col, source, at(row, side), side_send.at[col, source]).wait_send()
        forward(cross, source, at(row, side), side_send.at[cross, source]).wait_send()

        @pl.when(owner)
        def _():
            forward_half(x_here, source, at(row, cross), cross_send.at[1, source]).wait_send()
            forward_half(x_here, source, at(row, side), side_send.at[4 + x_here, source]).wait_send()
            forward_half(1 - x_here, source, at(row, side), side_send.at[5 - x_here, source]).wait_send()

        return carry

    lax.fori_loop(0, rows, finish, 0)
    for step in range(4):
        y_copy(tile_of(step)).wait_send()
    near_copy(0).wait_send()
    near_copy(1).wait_send()
    far_copy().wait_send()


def fused(factors, amplitudes, vir_energy, pair_energy):
    row_count, slab, aux = factors.shape
    vir = vir_energy.shape[0]
    rows = vir // row_count
    here_row = lax.axis_index("row")
    here_col = lax.axis_index("col")
    slabs = factors.transpose(1, 0, 2)
    mine = lax.dynamic_index_in_dim(amplitudes, here_col, 0, keepdims=False)
    mix = jnp.kron(mine, jnp.eye(SUB, dtype=mine.dtype))
    first = lax.dynamic_slice_in_dim(vir_energy, here_row * row_count, row_count)[:, None]
    pair = lax.dynamic_slice_in_dim(pair_energy, here_col, 1)[:, None]
    result = jax.ShapeDtypeStruct((1, row_count, vir), jnp.float32)
    dma = pltpu.SemaphoreType.DMA
    return pl.pallas_call(
        fused_kernel,
        in_specs=[pl.BlockSpec(memory_space=pltpu.VMEM)] * 5,
        out_specs=[pl.BlockSpec(memory_space=pltpu.VMEM)] * 2,
        out_shape=[result, result],
        scratch_shapes=[
            pltpu.VMEM((rows, slab, row_count, LANES), jnp.bfloat16),
            pltpu.VMEM((4, slab, row_count // 2, LANES), jnp.bfloat16),
            pltpu.VMEM((2, rows, slab, row_count // 2, LANES), jnp.bfloat16),
            pltpu.VMEM((5, slab, rows, row_count, LANES), jnp.bfloat16),
            pltpu.VMEM((5, rows, row_count, slab * LANES), jnp.bfloat16),
            pltpu.VMEM((rows // 2, 2, row_count, vir), jnp.float32),
            pltpu.VMEM((rows // 2, row_count, vir), jnp.float32),
            pltpu.VMEM((2, row_count, vir), jnp.float32),
            pltpu.VMEM((row_count, vir), jnp.float32),
            dma((rows,)),
            dma((4,)),
            dma((6, rows)),
            dma((2, rows)),
            dma((6, rows)),
            dma((rows // 2,)),
            dma((rows // 2,)),
            dma((2,)),
            dma((2,)),
            dma((1,)),
            dma((1,)),
        ],
        compiler_params=pltpu.CompilerParams(
            collective_id=0, has_side_effects=True, vmem_limit_bytes=52 * 1024 * 1024
        ),
        cost_estimate=pl.CostEstimate(
            flops=2 * vir * vir * slab * LANES * 5, bytes_accessed=4 * factors.size, transcendentals=0
        ),
    )(mix, slabs, first, vir_energy[None, :], pair)


def per_device(factors, amplitudes, vir_energy, pair_energy):
    row_count, slab, aux = factors.shape
    pairs = amplitudes.shape[0]
    vir = vir_energy.shape[0]
    rows = lax.axis_size("row")
    cols = lax.axis_size("col")
    here_row = lax.axis_index("row")
    here_col = lax.axis_index("col")
    share = pairs // cols
    if rows == 8 and cols == 4 and share == 1 and aux == 10 * LANES and row_count % (2 * SUB) == 0:
        return tuple(fused(factors, amplitudes, vir_energy, pair_energy))
    piece = aux // rows
    depth = piece * cols

    outgoing = factors.reshape(row_count, slab, rows, piece).transpose(2, 1, 0, 3)
    swapped = lax.all_to_all(outgoing, "row", split_axis=0, concat_axis=0, tiled=True)
    gathered = lax.all_gather(swapped, "col", axis=0, tiled=False)
    whole = gathered.transpose(2, 1, 3, 0, 4).reshape(slab, vir, depth)
    mine = lax.dynamic_slice_in_dim(amplitudes, here_col * share, share, 0)
    if depth % LANES == 0 and vir % 256 == 0:
        blocks = whole.reshape(slab, vir, depth // LANES, LANES).transpose(2, 0, 1, 3)
        partial = jnp.stack([ladder(blocks, mine[p]) for p in range(share)])
    else:
        mixed = jnp.einsum(
            "pcd,dbq->pcbq", mine, whole, preferred_element_type=jnp.float32
        ).astype(jnp.bfloat16)
        partial = jnp.einsum("caq,pcbq->pab", whole, mixed, preferred_element_type=jnp.float32)
    reduced = lax.psum_scatter(partial, "row", scatter_dimension=1, tiled=True)
    first_energy = lax.dynamic_slice_in_dim(vir_energy, here_row * row_count, row_count)
    pair_here = lax.dynamic_slice_in_dim(pair_energy, here_col * share, share)
    divisor = first_energy[None, :, None] + vir_energy[None, None, :] - pair_here[:, None, None]
    return (reduced, reduced / divisor)


def solution(mesh):
    return jax.shard_map(
        per_device,
        mesh=mesh,
        in_specs=(P("row", None, "col"), P(), P(), P()),
        out_specs=(P("col", "row", None), P("col", "row", None)),
        check_vma=False,
    )
```

```python
import jax
import jax.numpy as jnp
from jax import lax
from jax.experimental import pallas as pl
from jax.experimental.pallas import tpu as pltpu
from jax.sharding import PartitionSpec as P

LANES = 128
SUB = 16
GROUP = 8


def ladder_kernel(mix_ref, block_ref, out_ref, mixed):
    slab = block_ref.shape[1]
    vir = block_ref.shape[2]
    step = pl.program_id(0)

    @pl.when(step == 0)
    def _():
        out_ref[...] = jnp.zeros_like(out_ref)

    def mix(at, carry):
        first = pl.multiple_of(at * (SUB * GROUP), SUB * GROUP)
        wide = jnp.concatenate(
            [
                block_ref[0, :, pl.ds(first + j * SUB, SUB), :].reshape(slab * SUB, LANES)
                for j in range(GROUP)
            ],
            axis=1,
        )
        result = jnp.dot(mix_ref[...], wide, preferred_element_type=jnp.float32).astype(jnp.bfloat16)
        for j in range(GROUP):
            for c in range(slab):
                mixed[pl.ds(first + j * SUB, SUB), c * LANES : (c + 1) * LANES] = result[
                    c * SUB : (c + 1) * SUB, j * LANES : (j + 1) * LANES
                ]
        return carry

    lax.fori_loop(0, vir // (SUB * GROUP), mix, 0)

    tile = 256

    def multiply(at, carry):
        first = pl.multiple_of(at * tile, tile)
        left = jnp.concatenate([block_ref[0, c, pl.ds(first, tile), :] for c in range(slab)], axis=1)
        out_ref[pl.ds(first, tile), :] += lax.dot_general(
            left, mixed[...], (((1,), (1,)), ((), ())), preferred_element_type=jnp.float32
        )
        return carry

    lax.fori_loop(0, vir // tile, multiply, 0)


def ladder(blocks, amplitudes):
    count, slab, vir, _ = blocks.shape
    mix = jnp.kron(amplitudes, jnp.eye(SUB, dtype=amplitudes.dtype))
    return pl.pallas_call(
        ladder_kernel,
        grid=(count,),
        in_specs=[
            pl.BlockSpec((slab * SUB, slab * SUB), lambda i: (0, 0)),
            pl.BlockSpec((1, slab, vir, LANES), lambda i: (i, 0, 0, 0)),
        ],
        out_specs=pl.BlockSpec((vir, vir), lambda i: (0, 0)),
        out_shape=jax.ShapeDtypeStruct((vir, vir), jnp.float32),
        scratch_shapes=[pltpu.VMEM((vir, slab * LANES), jnp.bfloat16)],
        compiler_params=pltpu.CompilerParams(vmem_limit_bytes=32 * 1024 * 1024),
        cost_estimate=pl.CostEstimate(
            flops=2 * vir * vir * slab * LANES * count,
            bytes_accessed=2 * count * slab * vir * LANES,
            transcendentals=0,
        ),
    )(mix, blocks)


def flip(index, bits):
    low, mid, high = index % 2, (index // 2) % 2, index // 4
    b0, b1, b2 = bits % 2, (bits // 2) % 2, bits // 4
    return (low + b0) % 2 + 2 * ((mid + b1) % 2) + 4 * ((high + b2) % 2)


def fused_kernel(
    amplitude_ref,
    factors_ref,
    energy_ref,
    pair_ref,
    residual_ref,
    update_ref,
    blocks,
    packed,
    halves,
    held,
    mixed,
    mix_matrix,
    partial,
    y_in,
    near_in,
    far_in,
    row_send,
    extra_send,
    side_send,
    cross_send,
    arrive,
    y_send,
    y_arrive,
    near_send,
    near_arrive,
    far_send,
    far_arrive,
):
    row = lax.axis_index("row")
    col = lax.axis_index("col")
    slab, rows, row_count = held.shape[1], held.shape[2], held.shape[3]
    side = flip(col, 1)
    cross = flip(col, 2)
    corner = flip(col, 3)
    core, x_here = col % 2, col // 2
    y_here, z_here = row % 2, row // 2
    owner = core == y_here
    half_rows = row_count // 2
    low_lane = lax.broadcasted_iota(jnp.int32, (half_rows, LANES), 1) < LANES // 2

    def swap(value):
        return pltpu.roll(value, LANES // 2, 1)

    def at(row_id, col_id):
        return (row_id, col_id)

    barrier = pltpu.get_barrier_semaphore()
    peers = [at(flip(row, j), col) for j in range(1, rows)] + [at(row, side), at(row, cross)]
    for peer in peers:
        pl.semaphore_signal(barrier, inc=1, device_id=peer, device_id_type=pl.DeviceIdType.MESH)

    def cut(index):
        return factors_ref[:, :, pl.ds(pl.multiple_of(index * LANES, LANES), LANES)]

    def cut_for(j):
        other = flip(row, j)
        blocks[other] = cut(other)

    cut_for(4)
    cut_for(1)
    pl.semaphore_wait(barrier, len(peers))

    def remote(src, dst, send, recv, device):
        return pltpu.make_async_remote_copy(
            src_ref=src,
            dst_ref=dst,
            send_sem=send,
            recv_sem=recv,
            device_id=device,
            device_id_type=pl.DeviceIdType.MESH,
        )

    def row_copy(j):
        other = flip(row, j)
        return remote(
            blocks.at[other], held.at[col, :, row], row_send.at[j], arrive.at[col, row], at(other, col)
        )

    def extra_copy(d):
        target = flip(z_here, d)
        return remote(
            packed.at[target],
            halves.at[x_here, row],
            extra_send.at[d],
            arrive.at[4 + x_here, row],
            at(2 * target + core, col),
        )

    def forward(slot, source, device, send):
        return remote(held.at[slot, :, source], held.at[slot, :, source], send, arrive.at[slot, source], device)

    def forward_half(x, source, device, send):
        return remote(halves.at[x, source], halves.at[x, source], send, arrive.at[4 + x, source], device)

    def landed(slot, source):
        forward(slot, source, at(row, side), side_send.at[slot, source]).wait_recv()

    def landed_half(x, source):
        forward_half(x, source, at(row, side), side_send.at[4 + x, source]).wait_recv()

    row_copy(4).start()
    row_copy(1).start()
    for j in (2, 3):
        cut_for(j)
        row_copy(j).start()
    held[col, :, row] = cut(row)
    cut_for(5)
    row_copy(5).start()
    for t in range(4):
        start = (rows + t // 2) * LANES
        for c in range(slab):
            block = factors_ref[c, :, start : start + LANES].astype(jnp.float32)
            top, bottom = block[:half_rows], block[half_rows:]
            if t % 2 == 0:
                both = jnp.where(low_lane, top, swap(bottom))
            else:
                both = jnp.where(low_lane, swap(top), bottom)
            packed[t, c] = both.astype(jnp.bfloat16)

    @pl.when(owner)
    def _():
        halves[x_here, row] = packed[z_here]

    @pl.when(jnp.logical_not(owner))
    def _():
        extra_copy(0).start()

    extra_copy(1).start()
    extra_copy(2).start()
    cut_for(6)
    cut_for(7)

    def build_mix():
        wide = amplitude_ref[...].astype(jnp.float32)
        chosen = lax.broadcasted_iota(jnp.int32, wide.shape, 1) == col
        mine = jnp.sum(jnp.where(chosen, wide, 0.0), axis=1)
        lane = lax.broadcasted_iota(jnp.int32, (slab, slab * SUB), 1)
        spread = jnp.zeros((slab, slab * SUB), jnp.float32)
        for d in range(slab):
            spread = spread + jnp.where(lane // SUB == d, mine[:, d : d + 1], 0.0)
        square = (SUB, slab * SUB)
        same = lax.broadcasted_iota(jnp.int32, square, 0) == lax.broadcasted_iota(jnp.int32, square, 1) % SUB
        for c in range(slab):
            mix_matrix[c * SUB : (c + 1) * SUB, :] = jnp.where(same, spread[c : c + 1, :], 0.0).astype(jnp.bfloat16)

    def mix(slot, source):
        groups = row_count // SUB
        wide = jnp.concatenate(
            [
                held[slot, :, source, j * SUB : (j + 1) * SUB, :].reshape(slab * SUB, LANES)
                for j in range(groups)
            ],
            axis=1,
        )
        result = jnp.dot(mix_matrix[...], wide, preferred_element_type=jnp.float32).astype(jnp.bfloat16)
        for j in range(groups):
            for c in range(slab):
                mixed[slot, source, j * SUB : (j + 1) * SUB, c * LANES : (c + 1) * LANES] = result[
                    c * SUB : (c + 1) * SUB, j * LANES : (j + 1) * LANES
                ]

    def unpack(source):
        for c in range(slab):
            first = halves[0, source, c].astype(jnp.float32)
            second = halves[1, source, c].astype(jnp.float32)
            top = jnp.where(low_lane, first, swap(second))
            bottom = jnp.where(low_lane, swap(first), second)
            held[4, c, source, :half_rows] = top.astype(jnp.bfloat16)
            held[4, c, source, half_rows:] = bottom.astype(jnp.bfloat16)

    y_peer = flip(row, 1)
    own_half = z_here // 2

    def y_copy(d, half):
        tile = flip(z_here, d)
        return remote(
            partial.at[tile, half, 1 - y_here],
            y_in.at[tile, half],
            y_send.at[tile, half],
            y_arrive.at[tile, half],
            at(y_peer, col),
        )

    def near_copy(stage, half):
        return remote(
            partial.at[flip(z_here, 3 - 2 * stage), half, y_here],
            near_in.at[stage, half],
            near_send.at[stage, half],
            near_arrive.at[stage, half],
            at(flip(row, 2), col),
        )

    def far_copy(half):
        return remote(
            partial.at[flip(z_here, 2), half, y_here],
            far_in.at[half],
            far_send.at[half],
            far_arrive.at[half],
            at(flip(row, 4), col),
        )

    def multiply(d, half):
        tile = flip(z_here, d)

        def add_slot(slot, inner):
            left = jnp.concatenate(
                [held[slot, c, pl.ds(2 * tile, 2)].reshape(2 * row_count, LANES) for c in range(slab)], axis=1
            )
            right = mixed[slot, pl.ds(4 * half, 4)].reshape(4 * row_count, slab * LANES)
            product = lax.dot_general(
                left, right, (((1,), (1,)), ((), ())), preferred_element_type=jnp.float32
            ).reshape(2, row_count, 4 * row_count)

            @pl.when(slot == 0)
            def _():
                partial[tile, half] = product

            @pl.when(slot > 0)
            def _():
                partial[tile, half] += product

            return inner

        lax.fori_loop(0, 5, add_slot, 0)
        y_copy(d, half).start()

    def add_y(d, half):
        tile = flip(z_here, d)
        y_copy(d, half).wait_recv()
        partial[tile, half, y_here] += y_in[tile, half]

    def add_near(half):
        near_copy(0, half).wait_recv()
        partial[flip(z_here, 2), half, y_here] += near_in[0, half]
        far_copy(half).start()

    def gather_step(step, carry):
        @pl.when(step < rows)
        def _():
            source = flip(row, step)

            @pl.when(step > 0)
            def _():
                landed(col, source)

            forward(col, source, at(row, cross), cross_send.at[0, source]).start()
            forward(col, source, at(row, side), side_send.at[col, source]).start()

            @pl.when(owner)
            def _():
                @pl.when(step > 0)
                def _():
                    landed_half(x_here, source)

                forward_half(x_here, source, at(row, cross), cross_send.at[1, source]).start()
                forward_half(x_here, source, at(row, side), side_send.at[4 + x_here, source]).start()

        @pl.when(step == 0)
        def _():
            build_mix()

        @pl.when(step == 4)
        def _():
            row_copy(4).wait_send()
            row_copy(6).start()
            extra_copy(3).start()

        @pl.when(step == 5)
        def _():
            row_copy(5).wait_send()
            row_copy(7).start()

        @pl.when((step >= 1) & (step < rows + 1))
        def _():
            source = flip(row, step - 1)
            landed(cross, source)
            forward(cross, source, at(row, side), side_send.at[cross, source]).start()

            @pl.when(owner)
            def _():
                landed_half(1 - x_here, source)
                forward_half(1 - x_here, source, at(row, side), side_send.at[5 - x_here, source]).start()

        @pl.when(step >= 2)
        def _():
            source = flip(row, step - 2)
            landed(side, source)
            landed(corner, source)

            @pl.when(jnp.logical_not(owner))
            def _():
                landed_half(0, source)
                landed_half(1, source)

            unpack(source)

            def mix_slot(slot, inner):
                mix(slot, source)
                return inner

            lax.fori_loop(0, 5, mix_slot, 0)

        @pl.when(step == rows - 1)
        def _():
            def early(d, inner):
                multiply(d, own_half)
                return inner

            lax.fori_loop(0, 3, early, 0)

        return carry

    lax.fori_loop(0, rows + 2, gather_step, 0)

    def reduce_step(v, carry):
        @pl.when(v < 5)
        def _():
            first = (5 - v) // 5
            multiply(4 - v - first, flip(own_half, 1 - first))

        @pl.when(v == 0)
        def _():
            add_y(0, own_half)
            add_y(1, own_half)
            near_copy(1, own_half).start()
            add_y(2, own_half)

        @pl.when(v == 1)
        def _():
            add_y(3, own_half)
            near_copy(0, own_half).start()

        @pl.when(v == 2)
        def _():
            add_y(3, 1 - own_half)
            near_copy(0, 1 - own_half).start()
            add_near(own_half)

        @pl.when(v == 3)
        def _():
            add_y(2, 1 - own_half)
            add_near(1 - own_half)

        @pl.when(v == 4)
        def _():
            add_y(1, 1 - own_half)
            near_copy(1, 1 - own_half).start()

        @pl.when(v == 5)
        def _():
            add_y(0, 1 - own_half)

        return carry

    lax.fori_loop(0, 6, reduce_step, 0)

    across = energy_ref[...]
    here = lax.broadcasted_iota(jnp.int32, (row_count, rows * row_count), 1) == (
        lax.broadcasted_iota(jnp.int32, (row_count, rows * row_count), 0) + row * row_count
    )
    down = jnp.sum(jnp.where(here, across, 0.0), axis=1, keepdims=True)
    width = 4 * row_count
    for half in range(2):
        near_copy(1, half).wait_recv()
        far_copy(half).wait_recv()
        total = partial[z_here, half, y_here] + near_in[1, half] + far_in[half]
        span = slice(half * width, (half + 1) * width)
        residual_ref[0, :, span] = total
        update_ref[0, :, span] = total / (down + across[:, span] - pair_ref[col])

    for j in (1, 2, 3, 6, 7):
        row_copy(j).wait_send()

    @pl.when(jnp.logical_not(owner))
    def _():
        extra_copy(0).wait_send()

    for d in range(1, 4):
        extra_copy(d).wait_send()

    def finish(source, carry):
        forward(col, source, at(row, cross), cross_send.at[0, source]).wait_send()
        forward(col, source, at(row, side), side_send.at[col, source]).wait_send()
        forward(cross, source, at(row, side), side_send.at[cross, source]).wait_send()

        @pl.when(owner)
        def _():
            forward_half(x_here, source, at(row, cross), cross_send.at[1, source]).wait_send()
            forward_half(x_here, source, at(row, side), side_send.at[4 + x_here, source]).wait_send()
            forward_half(1 - x_here, source, at(row, side), side_send.at[5 - x_here, source]).wait_send()

        return carry

    lax.fori_loop(0, rows, finish, 0)
    for half in range(2):
        for d in range(4):
            y_copy(d, half).wait_send()
        near_copy(0, half).wait_send()
        near_copy(1, half).wait_send()
        far_copy(half).wait_send()


def fused(factors, amplitudes, vir_energy, pair_energy):
    row_count, slab, aux = factors.shape
    vir = vir_energy.shape[0]
    rows = vir // row_count
    slabs = factors.transpose(1, 0, 2)
    result = jax.ShapeDtypeStruct((1, row_count, vir), jnp.float32)
    dma = pltpu.SemaphoreType.DMA
    return pl.pallas_call(
        fused_kernel,
        in_specs=[pl.BlockSpec(memory_space=pltpu.VMEM)] * 3 + [pl.BlockSpec(memory_space=pltpu.SMEM)],
        out_specs=[pl.BlockSpec(memory_space=pltpu.VMEM)] * 2,
        out_shape=[result, result],
        scratch_shapes=[
            pltpu.VMEM((rows, slab, row_count, LANES), jnp.bfloat16),
            pltpu.VMEM((4, slab, row_count // 2, LANES), jnp.bfloat16),
            pltpu.VMEM((2, rows, slab, row_count // 2, LANES), jnp.bfloat16),
            pltpu.VMEM((5, slab, rows, row_count, LANES), jnp.bfloat16),
            pltpu.VMEM((5, rows, row_count, slab * LANES), jnp.bfloat16),
            pltpu.VMEM((slab * SUB, slab * SUB), jnp.bfloat16),
            pltpu.VMEM((rows // 2, 2, 2, row_count, vir // 2), jnp.float32),
            pltpu.VMEM((rows // 2, 2, row_count, vir // 2), jnp.float32),
            pltpu.VMEM((2, 2, row_count, vir // 2), jnp.float32),
            pltpu.VMEM((2, row_count, vir // 2), jnp.float32),
            dma((rows,)),
            dma((4,)),
            dma((6, rows)),
            dma((2, rows)),
            dma((6, rows)),
            dma((rows // 2, 2)),
            dma((rows // 2, 2)),
            dma((2, 2)),
            dma((2, 2)),
            dma((2,)),
            dma((2,)),
        ],
        compiler_params=pltpu.CompilerParams(
            collective_id=0, has_side_effects=True, vmem_limit_bytes=52 * 1024 * 1024
        ),
        cost_estimate=pl.CostEstimate(
            flops=2 * vir * vir * slab * LANES * 5, bytes_accessed=4 * factors.size, transcendentals=0
        ),
    )(amplitudes.transpose(1, 0, 2), slabs, vir_energy[None, :], pair_energy)


def per_device(factors, amplitudes, vir_energy, pair_energy):
    row_count, slab, aux = factors.shape
    pairs = amplitudes.shape[0]
    vir = vir_energy.shape[0]
    rows = lax.axis_size("row")
    cols = lax.axis_size("col")
    here_row = lax.axis_index("row")
    here_col = lax.axis_index("col")
    share = pairs // cols
    if rows == 8 and cols == 4 and share == 1 and aux == 10 * LANES and row_count % (2 * SUB) == 0:
        return tuple(fused(factors, amplitudes, vir_energy, pair_energy))
    piece = aux // rows
    depth = piece * cols

    outgoing = factors.reshape(row_count, slab, rows, piece).transpose(2, 1, 0, 3)
    swapped = lax.all_to_all(outgoing, "row", split_axis=0, concat_axis=0, tiled=True)
    gathered = lax.all_gather(swapped, "col", axis=0, tiled=False)
    whole = gathered.transpose(2, 1, 3, 0, 4).reshape(slab, vir, depth)
    mine = lax.dynamic_slice_in_dim(amplitudes, here_col * share, share, 0)
    if depth % LANES == 0 and vir % 256 == 0:
        blocks = whole.reshape(slab, vir, depth // LANES, LANES).transpose(2, 0, 1, 3)
        partial = jnp.stack([ladder(blocks, mine[p]) for p in range(share)])
    else:
        mixed = jnp.einsum(
            "pcd,dbq->pcbq", mine, whole, preferred_element_type=jnp.float32
        ).astype(jnp.bfloat16)
        partial = jnp.einsum("caq,pcbq->pab", whole, mixed, preferred_element_type=jnp.float32)
    reduced = lax.psum_scatter(partial, "row", scatter_dimension=1, tiled=True)
    first_energy = lax.dynamic_slice_in_dim(vir_energy, here_row * row_count, row_count)
    pair_here = lax.dynamic_slice_in_dim(pair_energy, here_col * share, share)
    divisor = first_energy[None, :, None] + vir_energy[None, None, :] - pair_here[:, None, None]
    return (reduced, reduced / divisor)


def solution(mesh):
    return jax.shard_map(
        per_device,
        mesh=mesh,
        in_specs=(P("row", None, "col"), P(), P(), P()),
        out_specs=(P("col", "row", None), P("col", "row", None)),
        check_vma=False,
    )
```

```python
import jax
import jax.numpy as jnp
from jax import lax
from jax.experimental import pallas as pl
from jax.experimental.pallas import tpu as pltpu
from jax.sharding import PartitionSpec as P

LANES = 128
SUB = 16
GROUP = 8


def ladder_kernel(mix_ref, block_ref, out_ref, mixed):
    slab = block_ref.shape[1]
    vir = block_ref.shape[2]
    step = pl.program_id(0)

    @pl.when(step == 0)
    def _():
        out_ref[...] = jnp.zeros_like(out_ref)

    def mix(at, carry):
        first = pl.multiple_of(at * (SUB * GROUP), SUB * GROUP)
        wide = jnp.concatenate(
            [
                block_ref[0, :, pl.ds(first + j * SUB, SUB), :].reshape(slab * SUB, LANES)
                for j in range(GROUP)
            ],
            axis=1,
        )
        result = jnp.dot(mix_ref[...], wide, preferred_element_type=jnp.float32).astype(jnp.bfloat16)
        for j in range(GROUP):
            for c in range(slab):
                mixed[pl.ds(first + j * SUB, SUB), c * LANES : (c + 1) * LANES] = result[
                    c * SUB : (c + 1) * SUB, j * LANES : (j + 1) * LANES
                ]
        return carry

    lax.fori_loop(0, vir // (SUB * GROUP), mix, 0)

    tile = 256

    def multiply(at, carry):
        first = pl.multiple_of(at * tile, tile)
        left = jnp.concatenate([block_ref[0, c, pl.ds(first, tile), :] for c in range(slab)], axis=1)
        out_ref[pl.ds(first, tile), :] += lax.dot_general(
            left, mixed[...], (((1,), (1,)), ((), ())), preferred_element_type=jnp.float32
        )
        return carry

    lax.fori_loop(0, vir // tile, multiply, 0)


def ladder(blocks, amplitudes):
    count, slab, vir, _ = blocks.shape
    mix = jnp.kron(amplitudes, jnp.eye(SUB, dtype=amplitudes.dtype))
    return pl.pallas_call(
        ladder_kernel,
        grid=(count,),
        in_specs=[
            pl.BlockSpec((slab * SUB, slab * SUB), lambda i: (0, 0)),
            pl.BlockSpec((1, slab, vir, LANES), lambda i: (i, 0, 0, 0)),
        ],
        out_specs=pl.BlockSpec((vir, vir), lambda i: (0, 0)),
        out_shape=jax.ShapeDtypeStruct((vir, vir), jnp.float32),
        scratch_shapes=[pltpu.VMEM((vir, slab * LANES), jnp.bfloat16)],
        compiler_params=pltpu.CompilerParams(vmem_limit_bytes=32 * 1024 * 1024),
        cost_estimate=pl.CostEstimate(
            flops=2 * vir * vir * slab * LANES * count,
            bytes_accessed=2 * count * slab * vir * LANES,
            transcendentals=0,
        ),
    )(mix, blocks)


def flip(index, bits):
    low, mid, high = index % 2, (index // 2) % 2, index // 4
    b0, b1, b2 = bits % 2, (bits // 2) % 2, bits // 4
    return (low + b0) % 2 + 2 * ((mid + b1) % 2) + 4 * ((high + b2) % 2)


def fused_kernel(
    amplitude_ref,
    factors_ref,
    energy_ref,
    pair_ref,
    residual_ref,
    update_ref,
    blocks,
    packed,
    halves,
    held,
    mixed,
    mix_matrix,
    partial,
    y_in,
    near_in,
    far_in,
    row_send,
    extra_send,
    side_send,
    cross_send,
    arrive,
    y_send,
    y_arrive,
    near_send,
    near_arrive,
    far_send,
    far_arrive,
):
    row = lax.axis_index("row")
    col = lax.axis_index("col")
    slab, rows, row_count = held.shape[1], held.shape[2], held.shape[3]
    side = flip(col, 1)
    cross = flip(col, 2)
    corner = flip(col, 3)
    core, x_here = col % 2, col // 2
    y_here, z_here = row % 2, row // 2
    owner = core == y_here
    half_rows = row_count // 2
    low_lane = lax.broadcasted_iota(jnp.int32, (half_rows, LANES), 1) < LANES // 2

    def swap(value):
        return pltpu.roll(value, LANES // 2, 1)

    def at(row_id, col_id):
        return (row_id, col_id)

    barrier = pltpu.get_barrier_semaphore()
    peers = [at(flip(row, j), col) for j in range(1, rows)] + [at(row, side), at(row, cross)]
    for peer in peers:
        pl.semaphore_signal(barrier, inc=1, device_id=peer, device_id_type=pl.DeviceIdType.MESH)

    def cut(index):
        return factors_ref[:, :, pl.ds(pl.multiple_of(index * LANES, LANES), LANES)]

    def cut_for(j):
        other = flip(row, j)
        blocks[other] = cut(other)

    cut_for(4)
    cut_for(1)
    pl.semaphore_wait(barrier, len(peers))

    def remote(src, dst, send, recv, device):
        return pltpu.make_async_remote_copy(
            src_ref=src,
            dst_ref=dst,
            send_sem=send,
            recv_sem=recv,
            device_id=device,
            device_id_type=pl.DeviceIdType.MESH,
        )

    def row_copy(j):
        other = flip(row, j)
        return remote(
            blocks.at[other], held.at[col, :, row], row_send.at[j], arrive.at[col, row], at(other, col)
        )

    def extra_copy(d):
        target = flip(z_here, d)
        return remote(
            packed.at[target],
            halves.at[x_here, row],
            extra_send.at[d],
            arrive.at[4 + x_here, row],
            at(2 * target + core, col),
        )

    def forward(slot, source, device, send):
        return remote(held.at[slot, :, source], held.at[slot, :, source], send, arrive.at[slot, source], device)

    def forward_half(x, source, device, send):
        return remote(halves.at[x, source], halves.at[x, source], send, arrive.at[4 + x, source], device)

    def landed(slot, source):
        forward(slot, source, at(row, side), side_send.at[slot, source]).wait_recv()

    def landed_half(x, source):
        forward_half(x, source, at(row, side), side_send.at[4 + x, source]).wait_recv()

    row_copy(4).start()
    row_copy(1).start()
    for j in (2, 3):
        cut_for(j)
        row_copy(j).start()
    held[col, :, row] = cut(row)
    cut_for(5)
    row_copy(5).start()
    for t in range(4):
        start = (rows + t // 2) * LANES
        for c in range(slab):
            block = factors_ref[c, :, start : start + LANES].astype(jnp.float32)
            top, bottom = block[:half_rows], block[half_rows:]
            if t % 2 == 0:
                both = jnp.where(low_lane, top, swap(bottom))
            else:
                both = jnp.where(low_lane, swap(top), bottom)
            packed[t, c] = both.astype(jnp.bfloat16)

    @pl.when(owner)
    def _():
        halves[x_here, row] = packed[z_here]

    @pl.when(jnp.logical_not(owner))
    def _():
        extra_copy(0).start()

    extra_copy(1).start()
    extra_copy(2).start()
    cut_for(6)
    cut_for(7)

    def build_mix():
        wide = amplitude_ref[...].astype(jnp.float32)
        chosen = lax.broadcasted_iota(jnp.int32, wide.shape, 1) == col
        mine = jnp.sum(jnp.where(chosen, wide, 0.0), axis=1)
        lane = lax.broadcasted_iota(jnp.int32, (slab, slab * SUB), 1)
        spread = jnp.zeros((slab, slab * SUB), jnp.float32)
        for d in range(slab):
            spread = spread + jnp.where(lane // SUB == d, mine[:, d : d + 1], 0.0)
        square = (SUB, slab * SUB)
        same = lax.broadcasted_iota(jnp.int32, square, 0) == lax.broadcasted_iota(jnp.int32, square, 1) % SUB
        for c in range(slab):
            mix_matrix[c * SUB : (c + 1) * SUB, :] = jnp.where(same, spread[c : c + 1, :], 0.0).astype(jnp.bfloat16)

    def mix(slot, source):
        groups = row_count // SUB
        wide = jnp.concatenate(
            [
                held[slot, :, source, j * SUB : (j + 1) * SUB, :].reshape(slab * SUB, LANES)
                for j in range(groups)
            ],
            axis=1,
        )
        result = jnp.dot(mix_matrix[...], wide, preferred_element_type=jnp.float32).astype(jnp.bfloat16)
        for j in range(groups):
            for c in range(slab):
                mixed[slot, source, j * SUB : (j + 1) * SUB, c * LANES : (c + 1) * LANES] = result[
                    c * SUB : (c + 1) * SUB, j * LANES : (j + 1) * LANES
                ]

    def unpack(source):
        for c in range(slab):
            first = halves[0, source, c].astype(jnp.float32)
            second = halves[1, source, c].astype(jnp.float32)
            top = jnp.where(low_lane, first, swap(second))
            bottom = jnp.where(low_lane, swap(first), second)
            held[4, c, source, :half_rows] = top.astype(jnp.bfloat16)
            held[4, c, source, half_rows:] = bottom.astype(jnp.bfloat16)

    y_peer = flip(row, 1)
    own_half = z_here // 2

    def y_copy(d, half):
        tile = flip(z_here, d)
        return remote(
            partial.at[tile, half, 1 - y_here],
            y_in.at[tile, half],
            y_send.at[tile, half],
            y_arrive.at[tile, half],
            at(y_peer, col),
        )

    def near_copy(stage, half):
        return remote(
            partial.at[flip(z_here, 3 - 2 * stage), half, y_here],
            near_in.at[stage, half],
            near_send.at[stage, half],
            near_arrive.at[stage, half],
            at(flip(row, 2), col),
        )

    def far_copy(half):
        return remote(
            partial.at[flip(z_here, 2), half, y_here],
            far_in.at[half],
            far_send.at[half],
            far_arrive.at[half],
            at(flip(row, 4), col),
        )

    def multiply(d, half):
        tile = flip(z_here, d)

        def add_slot(slot, inner):
            left = jnp.concatenate(
                [held[slot, c, pl.ds(2 * tile, 2)].reshape(2 * row_count, LANES) for c in range(slab)], axis=1
            )
            right = mixed[slot, pl.ds(4 * half, 4)].reshape(4 * row_count, slab * LANES)
            product = lax.dot_general(
                left, right, (((1,), (1,)), ((), ())), preferred_element_type=jnp.float32
            ).reshape(2, row_count, 4 * row_count)

            @pl.when(slot == 0)
            def _():
                partial[tile, half] = product

            @pl.when(slot > 0)
            def _():
                partial[tile, half] += product

            return inner

        lax.fori_loop(0, 5, add_slot, 0)
        y_copy(d, half).start()

    def add_y(d, half):
        tile = flip(z_here, d)
        y_copy(d, half).wait_recv()
        partial[tile, half, y_here] += y_in[tile, half]

    def add_near(half):
        near_copy(0, half).wait_recv()
        partial[flip(z_here, 2), half, y_here] += near_in[0, half]
        far_copy(half).start()

    def gather_step(step, carry):
        @pl.when(step < rows)
        def _():
            source = flip(row, step)

            @pl.when(step > 0)
            def _():
                landed(col, source)

            forward(col, source, at(row, cross), cross_send.at[0, source]).start()
            forward(col, source, at(row, side), side_send.at[col, source]).start()

            @pl.when(owner)
            def _():
                @pl.when(step > 0)
                def _():
                    landed_half(x_here, source)

                forward_half(x_here, source, at(row, cross), cross_send.at[1, source]).start()
                forward_half(x_here, source, at(row, side), side_send.at[4 + x_here, source]).start()

        @pl.when(step == 0)
        def _():
            build_mix()

        @pl.when(step == 2)
        def _():
            row_copy(6).start()
            extra_copy(3).start()

        @pl.when(step == 4)
        def _():
            row_copy(4).wait_send()
            row_copy(7).start()

        @pl.when(step == 5)
        def _():
            row_copy(5).wait_send()

        @pl.when((step >= 1) & (step < rows + 1))
        def _():
            source = flip(row, step - 1)
            landed(cross, source)
            forward(cross, source, at(row, side), side_send.at[cross, source]).start()

            @pl.when(owner)
            def _():
                landed_half(1 - x_here, source)
                forward_half(1 - x_here, source, at(row, side), side_send.at[5 - x_here, source]).start()

        @pl.when(step >= 2)
        def _():
            source = flip(row, step - 2)
            landed(side, source)
            landed(corner, source)

            @pl.when(jnp.logical_not(owner))
            def _():
                landed_half(0, source)
                landed_half(1, source)

            unpack(source)

            def mix_slot(slot, inner):
                mix(slot, source)
                return inner

            lax.fori_loop(0, 5, mix_slot, 0)

        @pl.when(step == rows - 1)
        def _():
            def early(d, inner):
                multiply(d, own_half)
                return inner

            lax.fori_loop(0, 3, early, 0)

        return carry

    lax.fori_loop(0, rows + 2, gather_step, 0)

    def reduce_step(v, carry):
        @pl.when(v < 5)
        def _():
            first = (5 - v) // 5
            multiply(4 - v - first, flip(own_half, 1 - first))

        @pl.when(v == 0)
        def _():
            add_y(0, own_half)
            add_y(1, own_half)
            near_copy(1, own_half).start()
            add_y(2, own_half)

        @pl.when(v == 1)
        def _():
            add_y(3, own_half)
            near_copy(0, own_half).start()

        @pl.when(v == 2)
        def _():
            add_y(3, 1 - own_half)
            near_copy(0, 1 - own_half).start()
            add_near(own_half)

        @pl.when(v == 3)
        def _():
            add_y(2, 1 - own_half)
            add_near(1 - own_half)

        @pl.when(v == 4)
        def _():
            add_y(1, 1 - own_half)
            near_copy(1, 1 - own_half).start()

        @pl.when(v == 5)
        def _():
            add_y(0, 1 - own_half)

        return carry

    lax.fori_loop(0, 6, reduce_step, 0)

    across = energy_ref[...]
    here = lax.broadcasted_iota(jnp.int32, (row_count, rows * row_count), 1) == (
        lax.broadcasted_iota(jnp.int32, (row_count, rows * row_count), 0) + row * row_count
    )
    down = jnp.sum(jnp.where(here, across, 0.0), axis=1, keepdims=True)
    width = 4 * row_count
    for half in range(2):
        near_copy(1, half).wait_recv()
        far_copy(half).wait_recv()
        total = partial[z_here, half, y_here] + near_in[1, half] + far_in[half]
        span = slice(half * width, (half + 1) * width)
        residual_ref[0, :, span] = total
        update_ref[0, :, span] = total / (down + across[:, span] - pair_ref[col])

    for j in (1, 2, 3, 6, 7):
        row_copy(j).wait_send()

    @pl.when(jnp.logical_not(owner))
    def _():
        extra_copy(0).wait_send()

    for d in range(1, 4):
        extra_copy(d).wait_send()

    def finish(source, carry):
        forward(col, source, at(row, cross), cross_send.at[0, source]).wait_send()
        forward(col, source, at(row, side), side_send.at[col, source]).wait_send()
        forward(cross, source, at(row, side), side_send.at[cross, source]).wait_send()

        @pl.when(owner)
        def _():
            forward_half(x_here, source, at(row, cross), cross_send.at[1, source]).wait_send()
            forward_half(x_here, source, at(row, side), side_send.at[4 + x_here, source]).wait_send()
            forward_half(1 - x_here, source, at(row, side), side_send.at[5 - x_here, source]).wait_send()

        return carry

    lax.fori_loop(0, rows, finish, 0)
    for half in range(2):
        for d in range(4):
            y_copy(d, half).wait_send()
        near_copy(0, half).wait_send()
        near_copy(1, half).wait_send()
        far_copy(half).wait_send()


def fused(factors, amplitudes, vir_energy, pair_energy):
    row_count, slab, aux = factors.shape
    vir = vir_energy.shape[0]
    rows = vir // row_count
    slabs = factors.transpose(1, 0, 2)
    result = jax.ShapeDtypeStruct((1, row_count, vir), jnp.float32)
    dma = pltpu.SemaphoreType.DMA
    return pl.pallas_call(
        fused_kernel,
        in_specs=[pl.BlockSpec(memory_space=pltpu.VMEM)] * 3 + [pl.BlockSpec(memory_space=pltpu.SMEM)],
        out_specs=[pl.BlockSpec(memory_space=pltpu.VMEM)] * 2,
        out_shape=[result, result],
        scratch_shapes=[
            pltpu.VMEM((rows, slab, row_count, LANES), jnp.bfloat16),
            pltpu.VMEM((4, slab, row_count // 2, LANES), jnp.bfloat16),
            pltpu.VMEM((2, rows, slab, row_count // 2, LANES), jnp.bfloat16),
            pltpu.VMEM((5, slab, rows, row_count, LANES), jnp.bfloat16),
            pltpu.VMEM((5, rows, row_count, slab * LANES), jnp.bfloat16),
            pltpu.VMEM((slab * SUB, slab * SUB), jnp.bfloat16),
            pltpu.VMEM((rows // 2, 2, 2, row_count, vir // 2), jnp.float32),
            pltpu.VMEM((rows // 2, 2, row_count, vir // 2), jnp.float32),
            pltpu.VMEM((2, 2, row_count, vir // 2), jnp.float32),
            pltpu.VMEM((2, row_count, vir // 2), jnp.float32),
            dma((rows,)),
            dma((4,)),
            dma((6, rows)),
            dma((2, rows)),
            dma((6, rows)),
            dma((rows // 2, 2)),
            dma((rows // 2, 2)),
            dma((2, 2)),
            dma((2, 2)),
            dma((2,)),
            dma((2,)),
        ],
        compiler_params=pltpu.CompilerParams(
            collective_id=0, has_side_effects=True, vmem_limit_bytes=52 * 1024 * 1024
        ),
        cost_estimate=pl.CostEstimate(
            flops=2 * vir * vir * slab * LANES * 5, bytes_accessed=4 * factors.size, transcendentals=0
        ),
    )(amplitudes.transpose(1, 0, 2), slabs, vir_energy[None, :], pair_energy)


def per_device(factors, amplitudes, vir_energy, pair_energy):
    row_count, slab, aux = factors.shape
    pairs = amplitudes.shape[0]
    vir = vir_energy.shape[0]
    rows = lax.axis_size("row")
    cols = lax.axis_size("col")
    here_row = lax.axis_index("row")
    here_col = lax.axis_index("col")
    share = pairs // cols
    if rows == 8 and cols == 4 and share == 1 and aux == 10 * LANES and row_count % (2 * SUB) == 0:
        return tuple(fused(factors, amplitudes, vir_energy, pair_energy))
    piece = aux // rows
    depth = piece * cols

    outgoing = factors.reshape(row_count, slab, rows, piece).transpose(2, 1, 0, 3)
    swapped = lax.all_to_all(outgoing, "row", split_axis=0, concat_axis=0, tiled=True)
    gathered = lax.all_gather(swapped, "col", axis=0, tiled=False)
    whole = gathered.transpose(2, 1, 3, 0, 4).reshape(slab, vir, depth)
    mine = lax.dynamic_slice_in_dim(amplitudes, here_col * share, share, 0)
    if depth % LANES == 0 and vir % 256 == 0:
        blocks = whole.reshape(slab, vir, depth // LANES, LANES).transpose(2, 0, 1, 3)
        partial = jnp.stack([ladder(blocks, mine[p]) for p in range(share)])
    else:
        mixed = jnp.einsum(
            "pcd,dbq->pcbq", mine, whole, preferred_element_type=jnp.float32
        ).astype(jnp.bfloat16)
        partial = jnp.einsum("caq,pcbq->pab", whole, mixed, preferred_element_type=jnp.float32)
    reduced = lax.psum_scatter(partial, "row", scatter_dimension=1, tiled=True)
    first_energy = lax.dynamic_slice_in_dim(vir_energy, here_row * row_count, row_count)
    pair_here = lax.dynamic_slice_in_dim(pair_energy, here_col * share, share)
    divisor = first_energy[None, :, None] + vir_energy[None, None, :] - pair_here[:, None, None]
    return (reduced, reduced / divisor)


def solution(mesh):
    return jax.shard_map(
        per_device,
        mesh=mesh,
        in_specs=(P("row", None, "col"), P(), P(), P()),
        out_specs=(P("col", "row", None), P("col", "row", None)),
        check_vma=False,
    )
```
